32 devices in a mesh: row: 8 (over y, x, core), col: 4 (over z).
Axes of the slice: x: 2, y: 2, z: 4, core: 2. Of those that a mesh axis runs over, the one named last changes fastest.
Arguments:
- inputs: bfloat16 [768, 12288], P(None, 'col'), may hold values from -6 to 6
- out_grad: bfloat16 [768, 12288], P(None, 'col'), may hold values from -6 to 6
- pre_act: bfloat16 [768, 24576], P('col', 'row'), may hold values from -8 to 8
- w_in: bfloat16 [12288, 24576], P('col', 'row'), may hold values from -0.0546875 to 0.0546875
- w_out: bfloat16 [24576, 12288], P('row', 'col'), may hold values from -0.0390625 to 0.0390625
Outputs:
- grad_inputs: bfloat16 [768, 12288], P('row', 'col')
- grad_w_in: bfloat16 [12288, 24576], P('col', 'row')
- grad_w_out: bfloat16 [24576, 12288], P('row', 'col')
The draws below stay inside these ranges and needn't reach their ends.
All inputs are finite; a program needn't handle non-finite values.
Results may differ from the reference program's by a relative error of at most 0.0049.
Values may be sent and summed in bfloat16 or wider, within the bound.
No kernel may reach another device: no remote copies, remote signals or barrier semaphores. Data moves between devices by JAX's collectives and lax.ppermute only.
A program may use at most 192 MiB of HBM per device.

```python
import math
import jax
import jax.numpy as jnp
from jax import lax

D = 12288
FW = 24576
TOKENS = 768


def level_of(key, shape, shards, smallest, largest):
    def one(dim, blocks):
        draws = jax.random.uniform(jax.random.fold_in(jax.random.fold_in(key, 6), dim), (blocks,), jnp.float32, smallest / len(shards), largest / len(shards))
        return jnp.repeat(jnp.exp(draws), shape[dim] // blocks).reshape((-1,) + (1,) * (len(shape) - dim - 1))

    gain = one(*shards[0])
    for cut in shards[1:]:
        gain = gain * one(*cut)
    return gain


def bell_draw(own_key, extent, width, most, shards=(), kind=jnp.bfloat16):
    array = width * jax.random.normal(own_key, extent, jnp.float32)
    if shards:
        array = array * level_of(own_key, extent, shards, -0.22, 0.18)
    return jnp.clip(array, -most, most).astype(kind)


def setup_inputs(seed: int = 0) -> dict:
    key_list = jax.random.split(jax.random.key(seed), 6)
    inputs = bell_draw(key_list[0], (TOKENS, D), 1.0, 6.0, ((1, 4),))
    out_grad = bell_draw(key_list[1], (TOKENS, D), 1.0, 6.0, ((1, 4),))
    pre_act = bell_draw(key_list[2], (TOKENS, FW), 1.5, 8.0, ((0, 4), (1, 8)))
    w_in = bell_draw(key_list[3], (D, FW), D ** -0.5, 0.0546875, ((0, 4), (1, 8)))
    w_out = bell_draw(key_list[4], (FW, D), FW ** -0.5, 0.0390625, ((0, 8), (1, 4)))
    return dict(inputs=inputs, out_grad=out_grad, pre_act=pre_act, w_in=w_in, w_out=w_out)


coef_c = math.sqrt(2.0 / math.pi)

def gelu_parts(pre_values):
    hval = pre_values.astype(jnp.float32)
    tval = jnp.tanh(coef_c * (hval + 0.044715 * hval * hval * hval))
    activ = 0.5 * hval * (1.0 + tval)
    deriv = 0.5 * (1.0 + tval) + 0.5 * hval * (1.0 - tval * tval) * coef_c * (1.0 + 3.0 * 0.044715 * hval * hval)
    return (activ, deriv)

def reference(inputs, out_grad, pre_act, w_in, w_out):
    scale_value = 1.0 / math.sqrt(TOKENS)
    act_grad = lax.dot_general(out_grad, w_out, (((1,), (1,)), ((), ())), preferred_element_type=jnp.float32)
    activ, deriv = gelu_parts(pre_act)
    activ = activ.astype(jnp.bfloat16)
    hid_grad = (act_grad * deriv).astype(jnp.bfloat16)
    grad_w_out = lax.dot_general(activ, out_grad, (((0,), (0,)), ((), ())), preferred_element_type=jnp.float32)
    grad_w_out = (grad_w_out * scale_value).astype(jnp.bfloat16)
    grad_w_in = lax.dot_general(inputs, hid_grad, (((0,), (0,)), ((), ())), preferred_element_type=jnp.float32)
    grad_w_in = (grad_w_in * scale_value).astype(jnp.bfloat16)
    grad_inputs = lax.dot_general(hid_grad, w_in, (((1,), (1,)), ((), ())), preferred_element_type=jnp.float32)
    return (grad_inputs.astype(jnp.bfloat16), grad_w_in, grad_w_out)
```

```python
import functools
import math

import jax
import jax.numpy as jnp
from jax import lax
from jax.experimental import pallas as pl
from jax.experimental.pallas import tpu as pltpu
from jax.sharding import PartitionSpec as P

coef_c = math.sqrt(2.0 / math.pi)
SMALL, LARGE = 26 * 1024 * 1024, 44 * 1024 * 1024
NT = (((1,), (1,)), ((), ()))
NN = (((1,), (0,)), ((), ()))


def gelu_parts(pre_values):
    hval = pre_values.astype(jnp.float32)
    tval = jnp.tanh(coef_c * (hval + 0.044715 * hval * hval * hval))
    activ = 0.5 * hval * (1.0 + tval)
    deriv = 0.5 * (1.0 + tval) + 0.5 * hval * (1.0 - tval * tval) * coef_c * (
        1.0 + 3.0 * 0.044715 * hval * hval
    )
    return (activ, deriv)


def dot32(a, b, dims):
    return lax.dot_general(a, b, dims, preferred_element_type=jnp.float32)


ANY = pl.BlockSpec(memory_space=pl.ANY)
TN = (((0,), (0,)), ((), ()))
TOKEN = jax.ShapeDtypeStruct((8, 128), jnp.float32)
SIDE, PLACE, OUTER, CORE, X, Y = range(6)


def call(body, place, steps, in_specs, out_specs, out_shapes, operands, after, scratch=(), aliases=None, vmem=SMALL):
    n_in, n_out = len(operands), len(out_shapes)

    def kernel(place_ref, *refs):
        outs = refs[n_in + 1:n_in + 1 + n_out]
        refs[n_in + 1 + n_out][...] = jnp.zeros((8, 128), jnp.float32)
        body(place_ref, *refs[:n_in], *outs, *refs[n_in + 2 + n_out:])

    return pl.pallas_call(
        kernel,
        grid_spec=pltpu.PrefetchScalarGridSpec(
            num_scalar_prefetch=1,
            grid=(steps,),
            in_specs=list(in_specs) + [ANY],
            out_specs=list(out_specs) + [pl.BlockSpec((8, 128), lambda i, s: (0, 0))],
            scratch_shapes=list(scratch),
        ),
        out_shape=list(out_shapes) + [TOKEN],
        input_output_aliases=aliases or {},
        compiler_params=pltpu.CompilerParams(vmem_limit_bytes=vmem, dimension_semantics=("arbitrary",)),
        cost_estimate=pl.CostEstimate(flops=0, bytes_accessed=0, transcendentals=0),
    )(place, *operands, after)


def shape16(*sizes):
    return jax.ShapeDtypeStruct(sizes, jnp.bfloat16)


def shape32(*sizes):
    return jax.ShapeDtypeStruct(sizes, jnp.float32)


def whole(*sizes):
    return pl.BlockSpec(sizes, lambda i, s: (0,) * len(sizes))


def choose(place_ref, which, put, ones, zeros):
    pl.when(place_ref[which] == 1)(lambda: put(ones))
    pl.when(place_ref[which] == 0)(lambda: put(zeros))


def act_partial(place, out_grad, w_out, start, width, after):
    tokens, model = out_grad.shape
    bw = 256

    def body(place_ref, grad, w, out):
        out[...] = dot32(grad[...], w[...], NT).astype(out.dtype)

    return call(
        body, place, width // bw,
        [whole(tokens, model), pl.BlockSpec((bw, model), lambda i, s: (start // bw + i, 0))],
        [pl.BlockSpec((tokens, bw), lambda i, s: (0, i))],
        [shape16(tokens, width)], (out_grad, w_out), after, vmem=LARGE,
    )


def own_piece(place, pre_act, start, width, after):
    rows = pre_act.shape[0]

    def body(place_ref, pre, out):
        out[...] = pre[...]

    return call(
        body, place, 1, [pl.BlockSpec((rows, width), lambda i, s: (0, start // width))], [whole(rows, width)],
        [shape16(rows, width)], (pre_act,), after,
    )


def near_half(place, own, other, after):
    rows, width = own.shape
    cut = width // 2

    def body(place_ref, mine, theirs, out):
        def put(pair):
            for k in range(2):
                for n, ref in enumerate(pair):
                    out[(2 * k + n) * rows:(2 * k + n + 1) * rows, :] = ref[:, k * cut:(k + 1) * cut]

        choose(place_ref, PLACE, put, (theirs, mine), (mine, theirs))

    return call(
        body, place, 1, [whole(rows, width)] * 2, [whole(4 * rows, cut)], [shape16(4 * rows, cut)],
        (own, other), after,
    )


def gate(place, value, after):
    return call(
        lambda *refs: None, place, 1, [ANY], [ANY], [jax.ShapeDtypeStruct(value.shape, value.dtype)],
        (value,), after, aliases={1: 0},
    )


def either(place, outers, inners, after):
    rows, width = inners.shape
    block = pl.BlockSpec((rows // 2, width), lambda i, s: (i, 0))

    def body(place_ref, a, b, out):
        def put(ref):
            out[...] = ref[...]

        choose(place_ref, OUTER, put, a, b)

    return call(body, place, 2, [block, block], [block], [shape16(rows, width)], (outers, inners), after)


def add_partials(place, mine, got, after):
    tokens, width = mine.shape

    def body(place_ref, a, b, out):
        out[...] = (a[...].astype(jnp.float32) + b[...].astype(jnp.float32)).astype(out.dtype)

    block = pl.BlockSpec((tokens // 2, width), lambda i, s: (i, 0))
    return call(body, place, 2, [block, block], [block], [shape16(tokens, width)], (mine, got), after)


def hid_part(place, mine, got, crossed, near, far, half_of, outers, after):
    tokens, width = mine.shape
    half = tokens // 2

    def body(place_ref, a, b, c, near_ref, far_ref, *rest):
        out = rest[-1]

        @pl.when(place_ref[OUTER] == 1)
        def _():
            out[...] = rest[0][...] if len(rest) == 2 else jnp.zeros_like(out)

        def fill(pre):
            total = a[...].astype(jnp.float32) + b[...].astype(jnp.float32) + c[...].astype(jnp.float32)
            out[...] = (total * gelu_parts(pre[...])[1]).astype(out.dtype)

        inner = place_ref[OUTER] == 0
        here = pl.program_id(0) == place_ref[SIDE]
        pl.when(inner & here)(lambda: fill(near_ref))
        pl.when(inner & jnp.logical_not(here))(lambda: fill(far_ref))

    block = pl.BlockSpec((half, width), lambda i, s: (i, 0))
    pre = pl.BlockSpec((half, width), lambda i, s: (half_of, 0))
    operands = [mine, got, crossed, near, far] + ([] if outers is None else [outers])
    specs = [block, block, block, pre, pre] + ([] if outers is None else [block])
    return call(body, place, 2, specs, [block], [shape16(tokens, width)], operands, after)


def out_weight(place, near, cross, got, half_of, out_grad, start, total, scale, into, after):
    tokens, width = near.shape
    half, model = tokens // 2, out_grad.shape[1]
    bd = 1024

    def body(place_ref, near_ref, cross_ref, got_ref, og_near, og_far, *rest):
        out, activ = rest[-2:]

        @pl.when(pl.program_id(0) == 0)
        def _():
            def fill(ref, first):
                for c in range(0, half, 128):
                    value = gelu_parts(ref[c:c + 128, :])[0]
                    activ[first + c:first + c + 128, :] = value.astype(activ.dtype)

            fill(near_ref, 0)
            choose(place_ref, OUTER, lambda ref: fill(ref, half), got_ref, cross_ref)

        value = dot32(activ[:half], og_near[...], TN) + dot32(activ[half:], og_far[...], TN)
        out[...] = (value * scale).astype(out.dtype)

    operands = [near, cross, got, out_grad, out_grad]
    specs = [pl.BlockSpec((half, width), lambda i, s: (half_of, 0))] * 3 + [
        pl.BlockSpec((half, bd), lambda i, s: (s[SIDE], i)),
        pl.BlockSpec((half, bd), lambda i, s: (1 - s[SIDE], i)),
    ]
    aliases = None
    if into is not None:
        operands.append(into)
        specs.append(ANY)
        aliases = {6: 0}
    assert start % width == 0
    return call(
        body, place, model // bd, specs,
        [pl.BlockSpec((width, bd), lambda i, s: (start // width, i))],
        [shape16(total, model)], operands, after,
        scratch=[pltpu.VMEM((tokens, width), jnp.bfloat16)], aliases=aliases,
    )


def join(place_ref, refs, hid):
    def put(parts):
        column = 0
        for ref in parts:
            width = ref.shape[1]
            hid[:, column:column + width] = ref[...]
            column += width

    choose(place_ref, OUTER, put, refs[1::2], refs[0::2])


def in_weight(place, inputs, parts, start, total, scale, into, after):
    tokens, model = inputs.shape
    flat = [part for pair in parts for part in pair]
    width = sum(part.shape[1] for part in flat) // 2
    bd = 1024

    def body(place_ref, x, *rest):
        out, hid = rest[-2:]
        pl.when(pl.program_id(0) == 0)(lambda: join(place_ref, rest[:len(flat)], hid))
        out[...] = (dot32(x[...], hid[...], TN) * scale).astype(out.dtype)

    operands = [inputs] + flat
    specs = [pl.BlockSpec((tokens, bd), lambda i, s: (0, i))] + [whole(*part.shape) for part in flat]
    aliases = None
    if into is not None:
        aliases = {1 + len(operands): 0}
        operands.append(into)
        specs.append(ANY)
    assert start % width == 0
    return call(
        body, place, model // bd, specs,
        [pl.BlockSpec((bd, width), lambda i, s: (i, start // width))],
        [shape16(model, total)], operands, after,
        scratch=[pltpu.VMEM((tokens, width), jnp.bfloat16)], aliases=aliases,
    )


def in_partial(place, parts, w_in, start, after):
    model = w_in.shape[0]
    flat = [part for pair in parts for part in pair]
    tokens = flat[0].shape[0]
    width = sum(part.shape[1] for part in flat) // 2
    bd = 512

    def body(place_ref, w, *rest):
        out, hid = rest[-2:]
        pl.when(pl.program_id(0) == 0)(lambda: join(place_ref, rest[:len(flat)], hid))
        out[...] = dot32(hid[...], w[...], NT)

    assert start % width == 0
    return call(
        body, place, model // bd,
        [pl.BlockSpec((bd, width), lambda i, s: (i, start // width))] + [whole(*part.shape) for part in flat],
        [pl.BlockSpec((tokens, bd), lambda i, s: (0, i))],
        [shape32(tokens, model)], [w_in] + flat, after,
        scratch=[pltpu.VMEM((tokens, width), jnp.bfloat16)], vmem=LARGE,
    )


def in_last(place, parts, w_in, start, total, after):
    model = w_in.shape[0]
    flat = [part for pair in parts for part in pair]
    tokens = flat[0].shape[0]
    width = sum(part.shape[1] for part in flat) // 2
    bd, size = 512, tokens // 8

    def body(place_ref, w, total_ref, *rest):
        keep, give, hid = rest[-3:]
        pl.when(pl.program_id(0) == 0)(lambda: join(place_ref, rest[:len(flat)], hid))
        value = dot32(hid[...], w[...], NT) + total_ref[...]

        def put(core):
            for k in range(4):
                rows = slice(k * size, (k + 1) * size)
                mine, theirs = (2 * k + core) * size, (2 * k + 1 - core) * size
                keep[rows, :] = value[mine:mine + size]
                give[rows, :] = value[theirs:theirs + size].astype(give.dtype)

        choose(place_ref, CORE, put, 1, 0)

    assert start % width == 0
    block = pl.BlockSpec((tokens // 2, bd), lambda i, s: (0, i))
    return call(
        body, place, model // bd,
        [
            pl.BlockSpec((bd, width), lambda i, s: (i, start // width)),
            pl.BlockSpec((tokens, bd), lambda i, s: (0, i)),
        ] + [whole(*part.shape) for part in flat],
        [block, block], [shape32(tokens // 2, model), shape16(tokens // 2, model)],
        [w_in, total] + flat, after, scratch=[pltpu.VMEM((tokens, width), jnp.bfloat16)], vmem=LARGE,
    )


def row_first(place, keep, got, after):
    rows, model = keep.shape
    size, cut = rows // 4, model // 2

    def body(place_ref, keep_ref, got_ref, keep_l, give_l, keep_r, give_r):
        def put(which):
            left, mine = which
            out, give = (keep_l, give_l) if left else (keep_r, give_r)
            for n in range(2):
                own, other = (2 * n + mine, 2 * n + 1 - mine) if left else (2 * mine + n, 2 * (1 - mine) + n)
                for k, ref in ((own, out), (other, give)):
                    part = slice(k * size, (k + 1) * size)
                    value = keep_ref[part, :] + got_ref[part, :].astype(jnp.float32)
                    ref[n * size:(n + 1) * size, :] = value.astype(ref.dtype)

        pl.when(pl.program_id(0) == 0)(lambda: choose(place_ref, X, put, (True, 1), (True, 0)))
        pl.when(pl.program_id(0) == 1)(lambda: choose(place_ref, Y, put, (False, 1), (False, 0)))

    block = pl.BlockSpec((rows, cut), lambda i, s: (0, i))
    return call(
        body, place, 2, [block, block], [whole(rows // 2, cut)] * 4,
        [shape32(rows // 2, cut), shape16(rows // 2, cut)] * 2, (keep, got), after,
    )


def row_second(place, keep_l, got_l, keep_r, got_r, after):
    rows, cut = keep_l.shape
    size = rows // 2

    def body(place_ref, *refs):
        for n, which in enumerate((Y, X)):
            keep_ref, got_ref, out, give = refs[2 * n], refs[2 * n + 1], refs[4 + 2 * n], refs[5 + 2 * n]

            def put(mine):
                for k, ref in ((mine, out), (1 - mine, give)):
                    part = slice(k * size, (k + 1) * size)
                    ref[...] = (keep_ref[part, :] + got_ref[part, :].astype(jnp.float32)).astype(ref.dtype)

            choose(place_ref, which, put, 1, 0)

    return call(
        body, place, 1, [whole(rows, cut)] * 4, [whole(size, cut)] * 4,
        [shape32(size, cut), shape16(size, cut)] * 2, (keep_l, got_l, keep_r, got_r), after,
    )


def row_third(place, keep_l, got_l, keep_r, got_r, after):
    size, cut = keep_l.shape

    def body(place_ref, a, b, c, d, out):
        out[:, :cut] = (a[...] + b[...].astype(jnp.float32)).astype(out.dtype)
        out[:, cut:] = (c[...] + d[...].astype(jnp.float32)).astype(out.dtype)

    return call(
        body, place, 1, [whole(size, cut)] * 4, [whole(size, 2 * cut)], [shape16(size, 2 * cut)],
        (keep_l, got_l, keep_r, got_r), after,
    )


ROW, COL = 8, 4
PAIRS = [(COL * r + c, COL * r + (c ^ 1)) for r in range(ROW) for c in range(COL)]
OUTWARD = [(COL * r + c, COL * r + (c ^ 1)) for r in range(ROW) for c in (0, 3)]
MIDDLE = [(COL * r + c, COL * r + 3 - c) for r in range(ROW) for c in (1, 2)] + [
    (COL * r + c, COL * (r ^ 1) + c) for r in range(ROW) for c in (0, 3)
]
WIDTH, PIECE = 512, 1024
WITH = {"I0": 1, "I1": 2, "C0": 3, "C1": 4, "C2": 5}
ORDER = (
    "O0", "O1", "O2", "A0", "N0", "A1", "N1", "I0", "B0", "N2", "A2", "I1", "A3", "A4", "V0", "B1", "C0", "V1", "B2",
    "A5", "C1", "V2", "B3", "W0", "C2", "B4", "V3", "C3", "W1", "W2", "B5", "C4", "W3", "C5", "T0", "I2", "T1", "W4",
    "R1", "W5", "V4", "R2", "V5", "R3",
)


def send(value, perm):
    return lax.ppermute(value, ("row", "col"), perm)


def swap(value, bit):
    return lax.ppermute(value, "row", [(i, i ^ bit) for i in range(ROW)])


def on_a_line(inputs, out_grad, pre_act, w_in, w_out):
    hidden = w_in.shape[1]
    scale = 1.0 / math.sqrt(inputs.shape[0])
    row, col = lax.axis_index("row"), lax.axis_index("col")
    outer = (col == 0) | (col == 3)
    place = jnp.stack([col // 2, col % 2, outer, row % 2, (row // 2) % 2, row // 4]).astype(jnp.int32)
    own, other, near, cross, far = {}, {}, {}, {}, {}
    share, got1, got2, hid, got3 = {}, {}, {}, {}, {}
    grad_w_in = grad_w_out = total = None
    after = jnp.zeros((8, 128), jnp.float32)
    for step in ORDER:
        kind, j = step[0], int(step[1:])
        out_with = WITH.get(step)
        if kind == "A":
            share[j], after = act_partial(place, out_grad, w_out, j * WIDTH, WIDTH, after)
            if j not in WITH.values():
                got1[j] = send(share[j], OUTWARD)
        elif kind == "O":
            own[j], after = own_piece(place, pre_act, j * PIECE, PIECE, after)
            other[j] = send(own[j], PAIRS)
        elif kind == "N":
            near[j], after = near_half(place, own[j], other[j], after)
            cross[j] = send(near[j], MIDDLE)
        elif kind == "I":
            if out_with is None:
                cross[j], after = gate(place, cross[j], after)
                far[j] = send(cross[j], PAIRS)
            else:
                both, after = either(place, share[out_with], cross[j], after)
                far[j] = got1[out_with] = send(both, PAIRS)
        elif kind == "B":
            both, after = add_partials(place, share[j], got1[j], after)
            got2[j] = send(both, MIDDLE)
        elif kind == "C":
            p, half_of = j * WIDTH // PIECE, j * WIDTH % PIECE // WIDTH
            outers = None if out_with is None else share[out_with]
            hid[j], after = hid_part(place, share[j], got1[j], got2[j], near[p], cross[p], half_of, outers, after)
            got3[j] = send(hid[j], PAIRS)
            if out_with is not None:
                got1[out_with] = got3[j]
        elif kind == "V":
            p, half_of = j * WIDTH // PIECE, j * WIDTH % PIECE // WIDTH
            grad_w_out, after = out_weight(
                place, near[p], cross[p], far[p], half_of, out_grad, j * WIDTH, hidden, scale, grad_w_out, after
            )
        elif kind == "W":
            grad_w_in, after = in_weight(
                place, inputs, [(hid[j], got3[j])], j * WIDTH, hidden, scale, grad_w_in, after
            )
        elif step == "T0":
            total, after = in_partial(place, [(hid[k], got3[k]) for k in (0, 1, 2, 3)], w_in, 0, after)
        elif step == "T1":
            parts = [(hid[k], got3[k]) for k in (4, 5)]
            keep, give, after = in_last(place, parts, w_in, 4 * WIDTH, total, after)
            got = swap(give, 1)
        elif step == "R1":
            keep_l, give_l, keep_r, give_r, after = row_first(place, keep, got, after)
            got_l, got_r = swap(give_l, 2), swap(give_r, 4)
        elif step == "R2":
            keep_l, give_l, keep_r, give_r, after = row_second(place, keep_l, got_l, keep_r, got_r, after)
            got_l, got_r = swap(give_l, 4), swap(give_r, 2)
        elif step == "R3":
            grad_inputs, after = row_third(place, keep_l, got_l, keep_r, got_r, after)
    return grad_inputs, grad_w_in, grad_w_out


def anywhere(inputs, out_grad, pre_act, w_in, w_out):
    scale = 1.0 / math.sqrt(inputs.shape[0])
    act_share = lax.psum_scatter(dot32(out_grad, w_out, NT), "col", scatter_dimension=0, tiled=True)
    local_act, local_deriv = gelu_parts(pre_act)
    hid_share = (act_share * local_deriv).astype(jnp.bfloat16)
    activ_all = lax.all_gather(local_act.astype(jnp.bfloat16), "col", axis=0, tiled=True)
    hid_all = lax.all_gather(hid_share, "col", axis=0, tiled=True)
    rows = (((0,), (0,)), ((), ()))
    grad_w_out = (dot32(activ_all, out_grad, rows) * scale).astype(jnp.bfloat16)
    grad_w_in = (dot32(inputs, hid_all, rows) * scale).astype(jnp.bfloat16)
    grad_inputs = lax.psum_scatter(dot32(hid_all, w_in, NT), "row", scatter_dimension=0, tiled=True)
    return (grad_inputs.astype(jnp.bfloat16), grad_w_in, grad_w_out)


def solution(mesh):
    placed = (P(None, "col"), P(None, "col"), P("col", "row"), P("col", "row"), P("row", "col"))
    line = mesh.shape["col"] == 4 and mesh.shape["row"] == 8
    return jax.shard_map(
        on_a_line if line else anywhere,
        mesh=mesh,
        in_specs=placed,
        out_specs=(P("row", "col"), P("col", "row"), P("row", "col")),
        check_vma=False,
    )
```

```python
import functools
import math

import jax
import jax.numpy as jnp
from jax import lax
from jax.experimental import pallas as pl
from jax.experimental.pallas import tpu as pltpu
from jax.sharding import PartitionSpec as P

coef_c = math.sqrt(2.0 / math.pi)
SMALL, LARGE = 26 * 1024 * 1024, 44 * 1024 * 1024
NT = (((1,), (1,)), ((), ()))
NN = (((1,), (0,)), ((), ()))


def gelu_parts(pre_values):
    hval = pre_values.astype(jnp.float32)
    tval = jnp.tanh(coef_c * (hval + 0.044715 * hval * hval * hval))
    activ = 0.5 * hval * (1.0 + tval)
    deriv = 0.5 * (1.0 + tval) + 0.5 * hval * (1.0 - tval * tval) * coef_c * (
        1.0 + 3.0 * 0.044715 * hval * hval
    )
    return (activ, deriv)


def dot32(a, b, dims):
    return lax.dot_general(a, b, dims, preferred_element_type=jnp.float32)


ANY = pl.BlockSpec(memory_space=pl.ANY)
TN = (((0,), (0,)), ((), ()))
TOKEN = jax.ShapeDtypeStruct((8, 128), jnp.float32)
SIDE, PLACE, OUTER, CORE, X, Y = range(6)


def call(body, place, steps, in_specs, out_specs, out_shapes, operands, after, scratch=(), aliases=None, vmem=SMALL):
    n_in, n_out = len(operands), len(out_shapes)

    def kernel(place_ref, *refs):
        outs = refs[n_in + 1:n_in + 1 + n_out]
        refs[n_in + 1 + n_out][...] = jnp.zeros((8, 128), jnp.float32)
        body(place_ref, *refs[:n_in], *outs, *refs[n_in + 2 + n_out:])

    return pl.pallas_call(
        kernel,
        grid_spec=pltpu.PrefetchScalarGridSpec(
            num_scalar_prefetch=1,
            grid=(steps,),
            in_specs=list(in_specs) + [ANY],
            out_specs=list(out_specs) + [pl.BlockSpec((8, 128), lambda i, s: (0, 0))],
            scratch_shapes=list(scratch),
        ),
        out_shape=list(out_shapes) + [TOKEN],
        input_output_aliases=aliases or {},
        compiler_params=pltpu.CompilerParams(vmem_limit_bytes=vmem, dimension_semantics=("arbitrary",)),
        cost_estimate=pl.CostEstimate(flops=0, bytes_accessed=0, transcendentals=0),
    )(place, *operands, after)


def shape16(*sizes):
    return jax.ShapeDtypeStruct(sizes, jnp.bfloat16)


def shape32(*sizes):
    return jax.ShapeDtypeStruct(sizes, jnp.float32)


def whole(*sizes):
    return pl.BlockSpec(sizes, lambda i, s: (0,) * len(sizes))


def choose(place_ref, which, put, ones, zeros):
    pl.when(place_ref[which] == 1)(lambda: put(ones))
    pl.when(place_ref[which] == 0)(lambda: put(zeros))


def act_partial(place, out_grad, w_out, start, after):
    tokens, model = out_grad.shape
    bw = 256
    per = WIDTH // bw

    def body(place_ref, grad, w, left, right):
        def put(out):
            out[...] = dot32(grad[...], w[...], NT).astype(out.dtype)

        pl.when(pl.program_id(0) < per)(lambda: put(left))
        pl.when(pl.program_id(0) >= per)(lambda: put(right))

    return call(
        body, place, 2 * per,
        [whole(tokens, model), pl.BlockSpec((bw, model), lambda i, s: (start // bw + i, 0))],
        [
            pl.BlockSpec((tokens, bw), lambda i, s: (0, jnp.minimum(i, per - 1))),
            pl.BlockSpec((tokens, bw), lambda i, s: (0, jnp.maximum(i - per, 0))),
        ],
        [shape16(tokens, WIDTH)] * 2, (out_grad, w_out), after, vmem=LARGE,
    )


def own_piece(place, pre_act, start, width, after):
    rows = pre_act.shape[0]

    def body(place_ref, pre, out):
        out[...] = pre[...]

    return call(
        body, place, 1, [pl.BlockSpec((rows, width), lambda i, s: (0, start // width))], [whole(rows, width)],
        [shape16(rows, width)], (pre_act,), after,
    )


def near_half(place, own, other, after):
    rows, width = own.shape
    cut = width // 2

    def body(place_ref, mine, theirs, out):
        def put(pair):
            for k in range(2):
                for n, ref in enumerate(pair):
                    out[(2 * k + n) * rows:(2 * k + n + 1) * rows, :] = ref[:, k * cut:(k + 1) * cut]

        choose(place_ref, PLACE, put, (theirs, mine), (mine, theirs))

    return call(
        body, place, 1, [whole(rows, width)] * 2, [whole(4 * rows, cut)], [shape16(4 * rows, cut)],
        (own, other), after,
    )


def near_and_relay(place, own, other, after):
    rows, width = own.shape
    cut = width // 2

    def body(place_ref, mine, theirs, out, relay):
        def put(pair):
            for k in range(2):
                for n, ref in enumerate(pair):
                    out[(2 * k + n) * rows:(2 * k + n + 1) * rows, :] = ref[:, k * cut:(k + 1) * cut]

        choose(place_ref, PLACE, put, (theirs, mine), (mine, theirs))
        relay[...] = theirs[...]

    return call(
        body, place, 1, [whole(rows, width)] * 2, [whole(4 * rows, cut), whole(rows, width)],
        [shape16(4 * rows, cut), shape16(rows, width)], (own, other), after,
    )


def gate(place, value, after):
    return call(
        lambda *refs: None, place, 1, [ANY], [ANY], [jax.ShapeDtypeStruct(value.shape, value.dtype)],
        (value,), after, aliases={1: 0},
    )


def either(place, outers, inners, after):
    rows, width = inners.shape
    block = pl.BlockSpec((rows // 2, width), lambda i, s: (i, 0))

    def body(place_ref, a, b, out):
        def put(ref):
            out[...] = ref[...]

        choose(place_ref, OUTER, put, a, b)

    return call(body, place, 2, [block, block], [block], [shape16(rows, width)], (outers, inners), after)


def add_partials(place, mine, got, after):
    tokens, width = mine.shape

    def body(place_ref, a, b, out):
        out[...] = (a[...].astype(jnp.float32) + b[...].astype(jnp.float32)).astype(out.dtype)

    block = pl.BlockSpec((tokens // 2, width), lambda i, s: (i, 0))
    return call(body, place, 2, [block, block], [block], [shape16(tokens, width)], (mine, got), after)


def hid_part(place, mine, got, crossed, near, far, half_of, outers, after):
    tokens, width = mine.shape
    half = tokens // 2

    def body(place_ref, a, b, c, near_ref, far_ref, *rest):
        out = rest[-1]

        @pl.when(place_ref[OUTER] == 1)
        def _():
            out[...] = rest[0][...] if len(rest) == 2 else jnp.zeros_like(out)

        def fill(pre):
            total = a[...].astype(jnp.float32) + b[...].astype(jnp.float32) + c[...].astype(jnp.float32)
            out[...] = (total * gelu_parts(pre[...])[1]).astype(out.dtype)

        inner = place_ref[OUTER] == 0
        here = pl.program_id(0) == place_ref[SIDE]
        pl.when(inner & here)(lambda: fill(near_ref))
        pl.when(inner & jnp.logical_not(here))(lambda: fill(far_ref))

    block = pl.BlockSpec((half, width), lambda i, s: (i, 0))
    pre = pl.BlockSpec((half, width), lambda i, s: (half_of, 0))
    operands = [mine, got, crossed, near, far] + ([] if outers is None else [outers])
    specs = [block, block, block, pre, pre] + ([] if outers is None else [block])
    return call(body, place, 2, specs, [block], [shape16(tokens, width)], operands, after)


def out_weight(place, near, cross, got, half_of, out_grad, start, total, scale, into, after):
    tokens, width = near.shape
    half, model = tokens // 2, out_grad.shape[1]
    bd = 1024

    def body(place_ref, near_ref, cross_ref, got_ref, grad, *rest):
        out, activ = rest[-2:]

        @pl.when(pl.program_id(0) == 0)
        def _():
            def fill(ref, first):
                for c in range(0, half, 128):
                    value = gelu_parts(ref[c:c + 128, :])[0]
                    rows = pl.ds(pl.multiple_of(first + c, 128), 128)
                    activ[rows, :] = value.astype(activ.dtype)

            here = place_ref[SIDE] * half
            fill(near_ref, here)
            choose(place_ref, OUTER, lambda ref: fill(ref, half - here), got_ref, cross_ref)

        out[...] = (dot32(activ[...], grad[...], TN) * scale).astype(out.dtype)

    operands = [near, cross, got, out_grad]
    specs = [pl.BlockSpec((half, width), lambda i, s: (half_of, 0))] * 3
    specs.append(pl.BlockSpec((tokens, bd), lambda i, s: (0, i)))
    aliases = None
    if into is not None:
        operands.append(into)
        specs.append(ANY)
        aliases = {5: 0}
    assert start % width == 0
    return call(
        body, place, model // bd, specs,
        [pl.BlockSpec((width, bd), lambda i, s: (start // width, i))],
        [shape16(total, model)], operands, after,
        scratch=[pltpu.VMEM((tokens, width), jnp.bfloat16)], aliases=aliases,
    )


def join(place_ref, refs, hid):
    def put(parts):
        column = 0
        for ref in parts:
            width = ref.shape[1]
            hid[:, column:column + width] = ref[...]
            column += width

    choose(place_ref, OUTER, put, refs[1::2], refs[0::2])


def in_weight(place, inputs, parts, start, total, scale, into, after):
    tokens, model = inputs.shape
    flat = [part for pair in parts for part in pair]
    width = sum(part.shape[1] for part in flat) // 2
    bd = 1024

    def body(place_ref, x, *rest):
        out, hid = rest[-2:]
        pl.when(pl.program_id(0) == 0)(lambda: join(place_ref, rest[:len(flat)], hid))
        out[...] = (dot32(x[...], hid[...], TN) * scale).astype(out.dtype)

    operands = [inputs] + flat
    specs = [pl.BlockSpec((tokens, bd), lambda i, s: (0, i))] + [whole(*part.shape) for part in flat]
    aliases = None
    if into is not None:
        aliases = {1 + len(operands): 0}
        operands.append(into)
        specs.append(ANY)
    assert start % width == 0
    return call(
        body, place, model // bd, specs,
        [pl.BlockSpec((bd, width), lambda i, s: (i, start // width))],
        [shape16(model, total)], operands, after,
        scratch=[pltpu.VMEM((tokens, width), jnp.bfloat16)], aliases=aliases,
    )


def in_partial(place, parts, w_in, start, after):
    model = w_in.shape[0]
    flat = [part for pair in parts for part in pair]
    tokens = flat[0].shape[0]
    width = sum(part.shape[1] for part in flat) // 2
    bd = 512

    def body(place_ref, w, *rest):
        out, hid = rest[-2:]
        pl.when(pl.program_id(0) == 0)(lambda: join(place_ref, rest[:len(flat)], hid))
        out[...] = dot32(hid[...], w[...], NT)

    assert start % width == 0
    return call(
        body, place, model // bd,
        [pl.BlockSpec((bd, width), lambda i, s: (i, start // width))] + [whole(*part.shape) for part in flat],
        [pl.BlockSpec((tokens, bd), lambda i, s: (0, i))],
        [shape32(tokens, model)], [w_in] + flat, after,
        scratch=[pltpu.VMEM((tokens, width), jnp.bfloat16)],
    )


def in_last(place, parts, w_in, start, total, after):
    model = w_in.shape[0]
    flat = [part for pair in parts for part in pair]
    tokens = flat[0].shape[0]
    width = sum(part.shape[1] for part in flat) // 2
    bd, size = 512, tokens // 8

    def body(place_ref, w, total_ref, *rest):
        keep, give, hid = rest[-3:]
        pl.when(pl.program_id(0) == 0)(lambda: join(place_ref, rest[:len(flat)], hid))
        value = dot32(hid[...], w[...], NT) + total_ref[...]

        def put(core):
            for k in range(4):
                rows = slice(k * size, (k + 1) * size)
                mine, theirs = (2 * k + core) * size, (2 * k + 1 - core) * size
                keep[rows, :] = value[mine:mine + size]
                give[rows, :] = value[theirs:theirs + size].astype(give.dtype)

        choose(place_ref, CORE, put, 1, 0)

    assert start % width == 0
    block = pl.BlockSpec((tokens // 2, bd), lambda i, s: (0, i))
    return call(
        body, place, model // bd,
        [
            pl.BlockSpec((bd, width), lambda i, s: (i, start // width)),
            pl.BlockSpec((tokens, bd), lambda i, s: (0, i)),
        ] + [whole(*part.shape) for part in flat],
        [block, block], [shape32(tokens // 2, model), shape16(tokens // 2, model)],
        [w_in, total] + flat, after, scratch=[pltpu.VMEM((tokens, width), jnp.bfloat16)], vmem=LARGE,
    )


def row_first(place, keep, got, after):
    rows, model = keep.shape
    size, cut = rows // 4, model // 2

    def body(place_ref, keep_ref, got_ref, keep_l, give_l, keep_r, give_r):
        def put(which):
            left, mine = which
            out, give = (keep_l, give_l) if left else (keep_r, give_r)
            for n in range(2):
                own, other = (2 * n + mine, 2 * n + 1 - mine) if left else (2 * mine + n, 2 * (1 - mine) + n)
                for k, ref in ((own, out), (other, give)):
                    part = slice(k * size, (k + 1) * size)
                    value = keep_ref[part, :] + got_ref[part, :].astype(jnp.float32)
                    ref[n * size:(n + 1) * size, :] = value.astype(ref.dtype)

        pl.when(pl.program_id(0) == 0)(lambda: choose(place_ref, X, put, (True, 1), (True, 0)))
        pl.when(pl.program_id(0) == 1)(lambda: choose(place_ref, Y, put, (False, 1), (False, 0)))

    block = pl.BlockSpec((rows, cut), lambda i, s: (0, i))
    return call(
        body, place, 2, [block, block], [whole(rows // 2, cut)] * 4,
        [shape32(rows // 2, cut), shape16(rows // 2, cut)] * 2, (keep, got), after,
    )


def row_second(place, keep_l, got_l, keep_r, got_r, after):
    rows, cut = keep_l.shape
    size = rows // 2

    def body(place_ref, *refs):
        for n, which in enumerate((Y, X)):
            keep_ref, got_ref, out, give = refs[2 * n], refs[2 * n + 1], refs[4 + 2 * n], refs[5 + 2 * n]

            def put(mine):
                for k, ref in ((mine, out), (1 - mine, give)):
                    part = slice(k * size, (k + 1) * size)
                    ref[...] = (keep_ref[part, :] + got_ref[part, :].astype(jnp.float32)).astype(ref.dtype)

            choose(place_ref, which, put, 1, 0)

    return call(
        body, place, 1, [whole(rows, cut)] * 4, [whole(size, cut)] * 4,
        [shape32(size, cut), shape16(size, cut)] * 2, (keep_l, got_l, keep_r, got_r), after,
    )


def row_third(place, keep_l, got_l, keep_r, got_r, after):
    size, cut = keep_l.shape

    def body(place_ref, a, b, c, d, out):
        out[:, :cut] = (a[...] + b[...].astype(jnp.float32)).astype(out.dtype)
        out[:, cut:] = (c[...] + d[...].astype(jnp.float32)).astype(out.dtype)

    return call(
        body, place, 1, [whole(size, cut)] * 4, [whole(size, 2 * cut)], [shape16(size, 2 * cut)],
        (keep_l, got_l, keep_r, got_r), after,
    )


ROW, COL = 8, 4
PAIRS = [(COL * r + c, COL * r + (c ^ 1)) for r in range(ROW) for c in range(COL)]
OUTWARD = [(COL * r + c, COL * r + (c ^ 1)) for r in range(ROW) for c in (0, 3)]
MIDDLE = [(COL * r + c, COL * r + 3 - c) for r in range(ROW) for c in (1, 2)] + [
    (COL * r + c, COL * (r ^ 1) + c) for r in range(ROW) for c in (0, 3)
]
WIDTH, PIECE = 512, 1024
WITH = {"I0": 1, "I1": 2, "C0": 3, "C1": 4, "C2": 5}
ORDER = (
    "O0", "O1", "A0", "N0", "A2", "Q0", "N1", "I0", "B0", "I1", "B1", "O2", "C0", "B2", "A4", "V0", "C1", "B3", "V1",
    "N2", "W0", "C2", "B4", "W1", "V2", "C3", "B5", "C4", "W2", "V3", "W3", "C5", "T0", "I2", "T1", "R1", "W4", "W5",
    "V4", "R2", "V5", "R3",
)


def send(value, perm):
    return lax.ppermute(value, ("row", "col"), perm)


def swap(value, bit):
    return lax.ppermute(value, "row", [(i, i ^ bit) for i in range(ROW)])


def on_a_line(inputs, out_grad, pre_act, w_in, w_out):
    hidden = w_in.shape[1]
    scale = 1.0 / math.sqrt(inputs.shape[0])
    row, col = lax.axis_index("row"), lax.axis_index("col")
    outer = (col == 0) | (col == 3)
    place = jnp.stack([col // 2, col % 2, outer, row % 2, (row // 2) % 2, row // 4]).astype(jnp.int32)
    own, other, near, cross, far = {}, {}, {}, {}, {}
    share, got1, got2, hid, got3 = {}, {}, {}, {}, {}
    grad_w_in = grad_w_out = total = None
    after = jnp.zeros((8, 128), jnp.float32)
    for step in ORDER:
        kind, j = step[0], int(step[1:])
        out_with = WITH.get(step)
        if kind == "A":
            share[j], share[j + 1], after = act_partial(place, out_grad, w_out, j * WIDTH, after)
            for k in (j, j + 1):
                if k not in WITH.values():
                    got1[k] = send(share[k], OUTWARD)
        elif kind == "O":
            own[j], after = own_piece(place, pre_act, j * PIECE, PIECE, after)
            other[j] = send(own[j], PAIRS)
            if j == 0:
                straight = send(own[j], MIDDLE)
        elif step == "N0":
            near[j], relay, after = near_and_relay(place, own[j], other[j], after)
            relay = send(relay, MIDDLE)
        elif step == "Q0":
            cross[j], after = near_half(place, relay, straight, after)
        elif kind == "N":
            near[j], after = near_half(place, own[j], other[j], after)
            cross[j] = send(near[j], MIDDLE)
        elif kind == "I":
            if out_with is None:
                cross[j], after = gate(place, cross[j], after)
                far[j] = send(cross[j], PAIRS)
            else:
                both, after = either(place, share[out_with], cross[j], after)
                far[j] = got1[out_with] = send(both, PAIRS)
        elif kind == "B":
            both, after = add_partials(place, share[j], got1[j], after)
            got2[j] = send(both, MIDDLE)
        elif kind == "C":
            p, half_of = j * WIDTH // PIECE, j * WIDTH % PIECE // WIDTH
            outers = None if out_with is None else share[out_with]
            hid[j], after = hid_part(place, share[j], got1[j], got2[j], near[p], cross[p], half_of, outers, after)
            got3[j] = send(hid[j], PAIRS)
            if out_with is not None:
                got1[out_with] = got3[j]
        elif kind == "V":
            p, half_of = j * WIDTH // PIECE, j * WIDTH % PIECE // WIDTH
            grad_w_out, after = out_weight(
                place, near[p], cross[p], far[p], half_of, out_grad, j * WIDTH, hidden, scale, grad_w_out, after
            )
        elif kind == "W":
            grad_w_in, after = in_weight(
                place, inputs, [(hid[j], got3[j])], j * WIDTH, hidden, scale, grad_w_in, after
            )
        elif step == "T0":
            total, after = in_partial(place, [(hid[k], got3[k]) for k in (0, 1, 2, 3)], w_in, 0, after)
        elif step == "T1":
            parts = [(hid[k], got3[k]) for k in (4, 5)]
            keep, give, after = in_last(place, parts, w_in, 4 * WIDTH, total, after)
            got = swap(give, 1)
        elif step == "R1":
            keep_l, give_l, keep_r, give_r, after = row_first(place, keep, got, after)
            got_l, got_r = swap(give_l, 2), swap(give_r, 4)
        elif step == "R2":
            keep_l, give_l, keep_r, give_r, after = row_second(place, keep_l, got_l, keep_r, got_r, after)
            got_l, got_r = swap(give_l, 4), swap(give_r, 2)
        elif step == "R3":
            grad_inputs, after = row_third(place, keep_l, got_l, keep_r, got_r, after)
    return grad_inputs, grad_w_in, grad_w_out


def anywhere(inputs, out_grad, pre_act, w_in, w_out):
    scale = 1.0 / math.sqrt(inputs.shape[0])
    act_share = lax.psum_scatter(dot32(out_grad, w_out, NT), "col", scatter_dimension=0, tiled=True)
    local_act, local_deriv = gelu_parts(pre_act)
    hid_share = (act_share * local_deriv).astype(jnp.bfloat16)
    activ_all = lax.all_gather(local_act.astype(jnp.bfloat16), "col", axis=0, tiled=True)
    hid_all = lax.all_gather(hid_share, "col", axis=0, tiled=True)
    rows = (((0,), (0,)), ((), ()))
    grad_w_out = (dot32(activ_all, out_grad, rows) * scale).astype(jnp.bfloat16)
    grad_w_in = (dot32(inputs, hid_all, rows) * scale).astype(jnp.bfloat16)
    grad_inputs = lax.psum_scatter(dot32(hid_all, w_in, NT), "row", scatter_dimension=0, tiled=True)
    return (grad_inputs.astype(jnp.bfloat16), grad_w_in, grad_w_out)


def solution(mesh):
    placed = (P(None, "col"), P(None, "col"), P("col", "row"), P("col", "row"), P("row", "col"))
    line = mesh.shape["col"] == 4 and mesh.shape["row"] == 8
    return jax.shard_map(
        on_a_line if line else anywhere,
        mesh=mesh,
        in_specs=placed,
        out_specs=(P("row", "col"), P("col", "row"), P("row", "col")),
        check_vma=False,
    )
```

```python
import functools
import math

import jax
import jax.numpy as jnp
from jax import lax
from jax.experimental import pallas as pl
from jax.experimental.pallas import tpu as pltpu
from jax.sharding import PartitionSpec as P

coef_c = math.sqrt(2.0 / math.pi)
SMALL, LARGE = 26 * 1024 * 1024, 44 * 1024 * 1024
NT = (((1,), (1,)), ((), ()))
NN = (((1,), (0,)), ((), ()))


def gelu_parts(pre_values):
    hval = pre_values.astype(jnp.float32)
    tval = jnp.tanh(coef_c * (hval + 0.044715 * hval * hval * hval))
    activ = 0.5 * hval * (1.0 + tval)
    deriv = 0.5 * (1.0 + tval) + 0.5 * hval * (1.0 - tval * tval) * coef_c * (
        1.0 + 3.0 * 0.044715 * hval * hval
    )
    return (activ, deriv)


def dot32(a, b, dims):
    return lax.dot_general(a, b, dims, preferred_element_type=jnp.float32)


ANY = pl.BlockSpec(memory_space=pl.ANY)
TN = (((0,), (0,)), ((), ()))
TOKEN = jax.ShapeDtypeStruct((8, 128), jnp.float32)
SIDE, PLACE, OUTER, CORE, X, Y = range(6)


def call(body, place, steps, in_specs, out_specs, out_shapes, operands, after, scratch=(), aliases=None, vmem=SMALL):
    n_in, n_out = len(operands), len(out_shapes)

    def kernel(place_ref, *refs):
        outs = refs[n_in + 1:n_in + 1 + n_out]
        refs[n_in + 1 + n_out][...] = jnp.zeros((8, 128), jnp.float32)
        body(place_ref, *refs[:n_in], *outs, *refs[n_in + 2 + n_out:])

    return pl.pallas_call(
        kernel,
        grid_spec=pltpu.PrefetchScalarGridSpec(
            num_scalar_prefetch=1,
            grid=(steps,),
            in_specs=list(in_specs) + [ANY],
            out_specs=list(out_specs) + [pl.BlockSpec((8, 128), lambda i, s: (0, 0))],
            scratch_shapes=list(scratch),
        ),
        out_shape=list(out_shapes) + [TOKEN],
        input_output_aliases=aliases or {},
        compiler_params=pltpu.CompilerParams(vmem_limit_bytes=vmem, dimension_semantics=("arbitrary",)),
        cost_estimate=pl.CostEstimate(flops=0, bytes_accessed=0, transcendentals=0),
    )(place, *operands, after)


def shape16(*sizes):
    return jax.ShapeDtypeStruct(sizes, jnp.bfloat16)


def shape32(*sizes):
    return jax.ShapeDtypeStruct(sizes, jnp.float32)


def whole(*sizes):
    return pl.BlockSpec(sizes, lambda i, s: (0,) * len(sizes))


def choose(place_ref, which, put, ones, zeros):
    pl.when(place_ref[which] == 1)(lambda: put(ones))
    pl.when(place_ref[which] == 0)(lambda: put(zeros))


def act_partial(place, out_grad, w_out, start, after):
    tokens, model = out_grad.shape
    bw = 256
    per = WIDTH // bw

    def body(place_ref, grad, w, left, right):
        def put(out):
            out[...] = dot32(grad[...], w[...], NT).astype(out.dtype)

        pl.when(pl.program_id(0) < per)(lambda: put(left))
        pl.when(pl.program_id(0) >= per)(lambda: put(right))

    return call(
        body, place, 2 * per,
        [whole(tokens, model), pl.BlockSpec((bw, model), lambda i, s: (start // bw + i, 0))],
        [
            pl.BlockSpec((tokens, bw), lambda i, s: (0, jnp.minimum(i, per - 1))),
            pl.BlockSpec((tokens, bw), lambda i, s: (0, jnp.maximum(i - per, 0))),
        ],
        [shape16(tokens, WIDTH)] * 2, (out_grad, w_out), after, vmem=LARGE,
    )


def own_piece(place, pre_act, start, width, after):
    rows = pre_act.shape[0]

    def body(place_ref, pre, out):
        out[...] = pre[...]

    return call(
        body, place, 1, [pl.BlockSpec((rows, width), lambda i, s: (0, start // width))], [whole(rows, width)],
        [shape16(rows, width)], (pre_act,), after,
    )


def near_half(place, own, other, after):
    rows, width = own.shape
    cut = width // 2

    def body(place_ref, mine, theirs, out):
        def put(pair):
            for k in range(2):
                for n, ref in enumerate(pair):
                    out[(2 * k + n) * rows:(2 * k + n + 1) * rows, :] = ref[:, k * cut:(k + 1) * cut]

        choose(place_ref, PLACE, put, (theirs, mine), (mine, theirs))

    return call(
        body, place, 1, [whole(rows, width)] * 2, [whole(4 * rows, cut)], [shape16(4 * rows, cut)],
        (own, other), after,
    )


def near_and_relay(place, own, other, after):
    rows, width = own.shape
    cut = width // 2

    def body(place_ref, mine, theirs, out, relay):
        def put(pair):
            for k in range(2):
                for n, ref in enumerate(pair):
                    out[(2 * k + n) * rows:(2 * k + n + 1) * rows, :] = ref[:, k * cut:(k + 1) * cut]

        choose(place_ref, PLACE, put, (theirs, mine), (mine, theirs))
        relay[...] = theirs[...]

    return call(
        body, place, 1, [whole(rows, width)] * 2, [whole(4 * rows, cut), whole(rows, width)],
        [shape16(4 * rows, cut), shape16(rows, width)], (own, other), after,
    )


def gate(place, value, after):
    return call(
        lambda *refs: None, place, 1, [ANY], [ANY], [jax.ShapeDtypeStruct(value.shape, value.dtype)],
        (value,), after, aliases={1: 0},
    )


def either(place, outers, inners, after):
    rows, width = inners.shape
    block = pl.BlockSpec((rows // 2, width), lambda i, s: (i, 0))

    def body(place_ref, a, b, out):
        def put(ref):
            out[...] = ref[...]

        choose(place_ref, OUTER, put, a, b)

    return call(body, place, 2, [block, block], [block], [shape16(rows, width)], (outers, inners), after)


def add_partials(place, mine, got, after):
    tokens, width = mine.shape

    def body(place_ref, a, b, out):
        out[...] = (a[...].astype(jnp.float32) + b[...].astype(jnp.float32)).astype(out.dtype)

    block = pl.BlockSpec((tokens // 2, width), lambda i, s: (i, 0))
    return call(body, place, 2, [block, block], [block], [shape16(tokens, width)], (mine, got), after)


def hid_part(place, mine, got, crossed, near, far, half_of, outers, after):
    tokens, width = mine.shape
    half = tokens // 2

    def body(place_ref, a, b, c, near_ref, far_ref, *rest):
        out = rest[-1]

        @pl.when(place_ref[OUTER] == 1)
        def _():
            out[...] = rest[0][...] if len(rest) == 2 else jnp.zeros_like(out)

        def fill(pre):
            total = a[...].astype(jnp.float32) + b[...].astype(jnp.float32) + c[...].astype(jnp.float32)
            out[...] = (total * gelu_parts(pre[...])[1]).astype(out.dtype)

        inner = place_ref[OUTER] == 0
        here = pl.program_id(0) == place_ref[SIDE]
        pl.when(inner & here)(lambda: fill(near_ref))
        pl.when(inner & jnp.logical_not(here))(lambda: fill(far_ref))

    block = pl.BlockSpec((half, width), lambda i, s: (i, 0))
    pre = pl.BlockSpec((half, width), lambda i, s: (half_of, 0))
    operands = [mine, got, crossed, near, far] + ([] if outers is None else [outers])
    specs = [block, block, block, pre, pre] + ([] if outers is None else [block])
    return call(body, place, 2, specs, [block], [shape16(tokens, width)], operands, after)


def out_weight(place, near, cross, got, half_of, out_grad, start, total, scale, into, after):
    tokens, width = near.shape
    half, model = tokens // 2, out_grad.shape[1]
    bd = 1024

    def body(place_ref, near_ref, cross_ref, got_ref, grad, *rest):
        out, activ = rest[-2:]

        @pl.when(pl.program_id(0) == 0)
        def _():
            def fill(ref, first):
                for c in range(0, half, 128):
                    value = gelu_parts(ref[c:c + 128, :])[0]
                    rows = pl.ds(pl.multiple_of(first + c, 128), 128)
                    activ[rows, :] = value.astype(activ.dtype)

            here = place_ref[SIDE] * half
            fill(near_ref, here)
            choose(place_ref, OUTER, lambda ref: fill(ref, half - here), got_ref, cross_ref)

        out[...] = (dot32(activ[...], grad[...], TN) * scale).astype(out.dtype)

    operands = [near, cross, got, out_grad]
    specs = [pl.BlockSpec((half, width), lambda i, s: (half_of, 0))] * 3
    specs.append(pl.BlockSpec((tokens, bd), lambda i, s: (0, i)))
    aliases = None
    if into is not None:
        operands.append(into)
        specs.append(ANY)
        aliases = {5: 0}
    assert start % width == 0
    return call(
        body, place, model // bd, specs,
        [pl.BlockSpec((width, bd), lambda i, s: (start // width, i))],
        [shape16(total, model)], operands, after,
        scratch=[pltpu.VMEM((tokens, width), jnp.bfloat16)], aliases=aliases,
    )


def join(place_ref, refs, hid):
    def put(parts):
        column = 0
        for ref in parts:
            width = ref.shape[1]
            hid[:, column:column + width] = ref[...]
            column += width

    choose(place_ref, OUTER, put, refs[1::2], refs[0::2])


def in_weight(place, inputs, parts, start, total, scale, into, after):
    tokens, model = inputs.shape
    flat = [part for pair in parts for part in pair]
    width = sum(part.shape[1] for part in flat) // 2
    bd = 1024

    def body(place_ref, x, *rest):
        out, hid = rest[-2:]
        pl.when(pl.program_id(0) == 0)(lambda: join(place_ref, rest[:len(flat)], hid))
        out[...] = (dot32(x[...], hid[...], TN) * scale).astype(out.dtype)

    operands = [inputs] + flat
    specs = [pl.BlockSpec((tokens, bd), lambda i, s: (0, i))] + [whole(*part.shape) for part in flat]
    aliases = None
    if into is not None:
        aliases = {1 + len(operands): 0}
        operands.append(into)
        specs.append(ANY)
    assert start % width == 0
    return call(
        body, place, model // bd, specs,
        [pl.BlockSpec((bd, width), lambda i, s: (i, start // width))],
        [shape16(model, total)], operands, after,
        scratch=[pltpu.VMEM((tokens, width), jnp.bfloat16)], aliases=aliases,
    )


def in_partial(place, parts, w_in, start, after):
    model = w_in.shape[0]
    flat = [part for pair in parts for part in pair]
    tokens = flat[0].shape[0]
    width = sum(part.shape[1] for part in flat) // 2
    bd = 512

    def body(place_ref, w, *rest):
        out, hid = rest[-2:]
        pl.when(pl.program_id(0) == 0)(lambda: join(place_ref, rest[:len(flat)], hid))
        out[...] = dot32(hid[...], w[...], NT)

    assert start % width == 0
    return call(
        body, place, model // bd,
        [pl.BlockSpec((bd, width), lambda i, s: (i, start // width))] + [whole(*part.shape) for part in flat],
        [pl.BlockSpec((tokens, bd), lambda i, s: (0, i))],
        [shape32(tokens, model)], [w_in] + flat, after,
        scratch=[pltpu.VMEM((tokens, width), jnp.bfloat16)], vmem=LARGE,
    )


def in_last(place, parts, w_in, start, total, after):
    model = w_in.shape[0]
    flat = [part for pair in parts for part in pair]
    tokens = flat[0].shape[0]
    width = sum(part.shape[1] for part in flat) // 2
    bd, size = 512, tokens // 8

    def body(place_ref, w, total_ref, *rest):
        keep, give, hid = rest[-3:]
        pl.when(pl.program_id(0) == 0)(lambda: join(place_ref, rest[:len(flat)], hid))
        value = dot32(hid[...], w[...], NT) + total_ref[...]

        def put(core):
            for k in range(4):
                rows = slice(k * size, (k + 1) * size)
                mine, theirs = (2 * k + core) * size, (2 * k + 1 - core) * size
                keep[rows, :] = value[mine:mine + size]
                give[rows, :] = value[theirs:theirs + size].astype(give.dtype)

        choose(place_ref, CORE, put, 1, 0)

    assert start % width == 0
    block = pl.BlockSpec((tokens // 2, bd), lambda i, s: (0, i))
    return call(
        body, place, model // bd,
        [
            pl.BlockSpec((bd, width), lambda i, s: (i, start // width)),
            pl.BlockSpec((tokens, bd), lambda i, s: (0, i)),
        ] + [whole(*part.shape) for part in flat],
        [block, block], [shape32(tokens // 2, model), shape16(tokens // 2, model)],
        [w_in, total] + flat, after, scratch=[pltpu.VMEM((tokens, width), jnp.bfloat16)], vmem=LARGE,
    )


def row_first(place, keep, got, after):
    rows, model = keep.shape
    size, cut = rows // 4, model // 2

    def body(place_ref, keep_ref, got_ref, keep_l, give_l, keep_r, give_r):
        def put(which):
            left, mine = which
            out, give = (keep_l, give_l) if left else (keep_r, give_r)
            for n in range(2):
                own, other = (2 * n + mine, 2 * n + 1 - mine) if left else (2 * mine + n, 2 * (1 - mine) + n)
                for k, ref in ((own, out), (other, give)):
                    part = slice(k * size, (k + 1) * size)
                    value = keep_ref[part, :] + got_ref[part, :].astype(jnp.float32)
                    ref[n * size:(n + 1) * size, :] = value.astype(ref.dtype)

        pl.when(pl.program_id(0) == 0)(lambda: choose(place_ref, X, put, (True, 1), (True, 0)))
        pl.when(pl.program_id(0) == 1)(lambda: choose(place_ref, Y, put, (False, 1), (False, 0)))

    block = pl.BlockSpec((rows, cut), lambda i, s: (0, i))
    return call(
        body, place, 2, [block, block], [whole(rows // 2, cut)] * 4,
        [shape32(rows // 2, cut), shape16(rows // 2, cut)] * 2, (keep, got), after,
    )


def row_second(place, keep_l, got_l, keep_r, got_r, after):
    rows, cut = keep_l.shape
    size = rows // 2

    def body(place_ref, *refs):
        for n, which in enumerate((Y, X)):
            keep_ref, got_ref, out, give = refs[2 * n], refs[2 * n + 1], refs[4 + 2 * n], refs[5 + 2 * n]

            def put(mine):
                for k, ref in ((mine, out), (1 - mine, give)):
                    part = slice(k * size, (k + 1) * size)
                    ref[...] = (keep_ref[part, :] + got_ref[part, :].astype(jnp.float32)).astype(ref.dtype)

            choose(place_ref, which, put, 1, 0)

    return call(
        body, place, 1, [whole(rows, cut)] * 4, [whole(size, cut)] * 4,
        [shape32(size, cut), shape16(size, cut)] * 2, (keep_l, got_l, keep_r, got_r), after,
    )


def row_third(place, keep_l, got_l, keep_r, got_r, after):
    size, cut = keep_l.shape

    def body(place_ref, a, b, c, d, out):
        out[:, :cut] = (a[...] + b[...].astype(jnp.float32)).astype(out.dtype)
        out[:, cut:] = (c[...] + d[...].astype(jnp.float32)).astype(out.dtype)

    return call(
        body, place, 1, [whole(size, cut)] * 4, [whole(size, 2 * cut)], [shape16(size, 2 * cut)],
        (keep_l, got_l, keep_r, got_r), after,
    )


ROW, COL = 8, 4
PAIRS = [(COL * r + c, COL * r + (c ^ 1)) for r in range(ROW) for c in range(COL)]
OUTWARD = [(COL * r + c, COL * r + (c ^ 1)) for r in range(ROW) for c in (0, 3)]
MIDDLE = [(COL * r + c, COL * r + 3 - c) for r in range(ROW) for c in (1, 2)] + [
    (COL * r + c, COL * (r ^ 1) + c) for r in range(ROW) for c in (0, 3)
]
WIDTH, PIECE = 512, 1024
WITH = {"I0": 1, "I1": 2, "C0": 3, "C1": 4, "C2": 5}
ORDER = (
    "O0", "O1", "A0", "N0", "A2", "Q0", "N1", "I0", "B0", "I1", "B1", "O2", "C0", "B2", "A4", "V0", "C1", "B3", "V1",
    "N2", "W0", "C2", "B4", "W1", "V2", "C3", "B5", "W2", "V3", "C4", "T0", "C5", "W3", "I2", "W4", "T1", "R1", "W5",
    "V4", "R2", "V5", "R3",
)


def send(value, perm):
    return lax.ppermute(value, ("row", "col"), perm)


def swap(value, bit):
    return lax.ppermute(value, "row", [(i, i ^ bit) for i in range(ROW)])


def on_a_line(inputs, out_grad, pre_act, w_in, w_out):
    hidden = w_in.shape[1]
    scale = 1.0 / math.sqrt(inputs.shape[0])
    row, col = lax.axis_index("row"), lax.axis_index("col")
    outer = (col == 0) | (col == 3)
    place = jnp.stack([col // 2, col % 2, outer, row % 2, (row // 2) % 2, row // 4]).astype(jnp.int32)
    own, other, near, cross, far = {}, {}, {}, {}, {}
    share, got1, got2, hid, got3 = {}, {}, {}, {}, {}
    grad_w_in = grad_w_out = total = None
    after = jnp.zeros((8, 128), jnp.float32)
    for step in ORDER:
        kind, j = step[0], int(step[1:])
        out_with = WITH.get(step)
        if kind == "A":
            share[j], share[j + 1], after = act_partial(place, out_grad, w_out, j * WIDTH, after)
            for k in (j, j + 1):
                if k not in WITH.values():
                    got1[k] = send(share[k], OUTWARD)
        elif kind == "O":
            own[j], after = own_piece(place, pre_act, j * PIECE, PIECE, after)
            other[j] = send(own[j], PAIRS)
            if j == 0:
                straight = send(own[j], MIDDLE)
        elif step == "N0":
            near[j], relay, after = near_and_relay(place, own[j], other[j], after)
            relay = send(relay, MIDDLE)
        elif step == "Q0":
            cross[j], after = near_half(place, relay, straight, after)
        elif kind == "N":
            near[j], after = near_half(place, own[j], other[j], after)
            cross[j] = send(near[j], MIDDLE)
        elif kind == "I":
            if out_with is None:
                cross[j], after = gate(place, cross[j], after)
                far[j] = send(cross[j], PAIRS)
            else:
                both, after = either(place, share[out_with], cross[j], after)
                far[j] = got1[out_with] = send(both, PAIRS)
        elif kind == "B":
            both, after = add_partials(place, share[j], got1[j], after)
            got2[j] = send(both, MIDDLE)
        elif kind == "C":
            p, half_of = j * WIDTH // PIECE, j * WIDTH % PIECE // WIDTH
            outers = None if out_with is None else share[out_with]
            hid[j], after = hid_part(place, share[j], got1[j], got2[j], near[p], cross[p], half_of, outers, after)
            got3[j] = send(hid[j], PAIRS)
            if out_with is not None:
                got1[out_with] = got3[j]
        elif kind == "V":
            p, half_of = j * WIDTH // PIECE, j * WIDTH % PIECE // WIDTH
            grad_w_out, after = out_weight(
                place, near[p], cross[p], far[p], half_of, out_grad, j * WIDTH, hidden, scale, grad_w_out, after
            )
        elif kind == "W":
            grad_w_in, after = in_weight(
                place, inputs, [(hid[j], got3[j])], j * WIDTH, hidden, scale, grad_w_in, after
            )
        elif step == "T0":
            total, after = in_partial(place, [(hid[k], got3[k]) for k in (0, 1, 2, 3)], w_in, 0, after)
        elif step == "T1":
            parts = [(hid[k], got3[k]) for k in (4, 5)]
            keep, give, after = in_last(place, parts, w_in, 4 * WIDTH, total, after)
            got = swap(give, 1)
        elif step == "R1":
            keep_l, give_l, keep_r, give_r, after = row_first(place, keep, got, after)
            got_l, got_r = swap(give_l, 2), swap(give_r, 4)
        elif step == "R2":
            keep_l, give_l, keep_r, give_r, after = row_second(place, keep_l, got_l, keep_r, got_r, after)
            got_l, got_r = swap(give_l, 4), swap(give_r, 2)
        elif step == "R3":
            grad_inputs, after = row_third(place, keep_l, got_l, keep_r, got_r, after)
    return grad_inputs, grad_w_in, grad_w_out


def anywhere(inputs, out_grad, pre_act, w_in, w_out):
    scale = 1.0 / math.sqrt(inputs.shape[0])
    act_share = lax.psum_scatter(dot32(out_grad, w_out, NT), "col", scatter_dimension=0, tiled=True)
    local_act, local_deriv = gelu_parts(pre_act)
    hid_share = (act_share * local_deriv).astype(jnp.bfloat16)
    activ_all = lax.all_gather(local_act.astype(jnp.bfloat16), "col", axis=0, tiled=True)
    hid_all = lax.all_gather(hid_share, "col", axis=0, tiled=True)
    rows = (((0,), (0,)), ((), ()))
    grad_w_out = (dot32(activ_all, out_grad, rows) * scale).astype(jnp.bfloat16)
    grad_w_in = (dot32(inputs, hid_all, rows) * scale).astype(jnp.bfloat16)
    grad_inputs = lax.psum_scatter(dot32(hid_all, w_in, NT), "row", scatter_dimension=0, tiled=True)
    return (grad_inputs.astype(jnp.bfloat16), grad_w_in, grad_w_out)


def solution(mesh):
    placed = (P(None, "col"), P(None, "col"), P("col", "row"), P("col", "row"), P("row", "col"))
    line = mesh.shape["col"] == 4 and mesh.shape["row"] == 8
    return jax.shard_map(
        on_a_line if line else anywhere,
        mesh=mesh,
        in_specs=placed,
        out_specs=(P("row", "col"), P("col", "row"), P("row", "col")),
        check_vma=False,
    )
```
